32 devices in a mesh: dp: 8 (over z, x), proto: 4 (over y, core).
Axes of the slice: x: 2, y: 2, z: 4, core: 2. Of those that a mesh axis runs over, the one named last changes fastest.
Arguments:
- teacher_feat: bfloat16 [4096, 256], P('dp'), may hold values from -16 to 16
- student_feat: bfloat16 [4096, 256], P('dp'), may hold values from -16 to 16
- teacher_protos: bfloat16 [65536, 256], P('proto'), may hold values from -16 to 16
- student_protos: bfloat16 [65536, 256], P('proto'), may hold values from -16 to 16
Outputs:
- row_loss: float32 [4096], P('dp')
- feature_grad: bfloat16 [4096, 256], P('dp')
- proto_grad: bfloat16 [65536, 256], P(('proto', 'dp'))
The draws below stay inside these ranges and needn't reach their ends.
All inputs are finite; a program needn't handle non-finite values.
Results may differ from the reference program's by a relative error of at most 0.0069.
Values may be sent and summed in bfloat16 or wider, within the bound.
A program may use at most 192 MiB of HBM per device.

```python
import math
import jax
import jax.numpy as jnp
from jax import lax

DIM = 256
PROTOS = 65536
ITERS = 3
BATCH = 4096


def shared_centers(key):
    return jax.random.truncated_normal(jax.random.fold_in(key, 900), -4.0, 4.0, (64, DIM))


def proto_signal(key):
    centers = shared_centers(key)
    inner = jax.random.fold_in(key, 910)
    k_ids, k_str = jax.random.split(inner)
    ids = jax.random.randint(k_ids, (PROTOS,), 0, 64)
    strength = jnp.exp(jax.random.uniform(k_str, (PROTOS, 1), minval=jnp.log(0.3), maxval=jnp.log(3.0)))
    return strength * centers[ids]


def feature_signal(key):
    centers = shared_centers(key)
    inner = jax.random.fold_in(key, 920)
    k_ids, k_str = jax.random.split(inner)
    ids = jax.random.randint(k_ids, (BATCH,), 0, 64)
    strength = jnp.exp(jax.random.uniform(k_str, (BATCH, 1), minval=jnp.log(0.3), maxval=jnp.log(3.0)))
    return strength * centers[ids]


def draw_teacher_feat(key, part):
    signal = feature_signal(key)
    key = jax.random.fold_in(key, 1)
    noise = jax.random.truncated_normal(key, -4.0, 4.0, (BATCH, DIM))
    return (signal + noise).astype(jnp.bfloat16)


def draw_student_feat(key, part):
    signal = feature_signal(key)
    key = jax.random.fold_in(key, 2)
    noise = jax.random.truncated_normal(key, -4.0, 4.0, (BATCH, DIM))
    return (signal + noise).astype(jnp.bfloat16)


def draw_teacher_protos(key, part):
    signal = proto_signal(key)
    key = jax.random.fold_in(key, 3)
    noise = jax.random.truncated_normal(key, -4.0, 4.0, (PROTOS, DIM))
    return (signal + noise).astype(jnp.bfloat16)


def draw_student_protos(key, part):
    signal = proto_signal(key)
    key = jax.random.fold_in(key, 4)
    noise = jax.random.truncated_normal(key, -4.0, 4.0, (PROTOS, DIM))
    return (signal + noise).astype(jnp.bfloat16)


def setup_inputs(seed: int = 0) -> dict:
    keys = jax.random.split(jax.random.key(seed), 5)
    teacher_feat = draw_teacher_feat(jax.random.fold_in(keys[4], 71), 0)
    student_feat = draw_student_feat(jax.random.fold_in(keys[4], 71), 0)
    teacher_protos = draw_teacher_protos(jax.random.fold_in(keys[4], 71), 0)
    student_protos = draw_student_protos(jax.random.fold_in(keys[4], 71), 0)
    return dict(teacher_feat=teacher_feat, student_feat=student_feat, teacher_protos=teacher_protos, student_protos=student_protos)


teacher_temp = 0.07
student_temp = 0.1

def unit_rows(x):
    xf = x.astype(jnp.float32)
    return (xf * lax.rsqrt(lax.optimization_barrier(jnp.sum(xf * xf, axis=1, keepdims=True)) + 1e-06)).astype(jnp.bfloat16)

def by_rows(left, right):
    return lax.dot_general(left, right, (((1,), (1,)), ((), ())), preferred_element_type=jnp.float32)

def reference(teacher_feat, student_feat, teacher_protos, student_protos):
    t_unit = unit_rows(teacher_feat)
    s_unit = unit_rows(student_feat)
    t_dirs = unit_rows(teacher_protos)
    s_dirs = unit_rows(student_protos)
    block = math.gcd(BATCH, 1024)
    count = BATCH // block
    t_blocks = t_unit.reshape(count, block, DIM)
    s_blocks = s_unit.reshape(count, block, DIM)

    def expo_of(tb):
        return jnp.exp(by_rows(tb, t_dirs) / teacher_temp)
    row_scale = jnp.ones((count, block), jnp.float32)
    col_scale = jnp.ones((PROTOS,), jnp.float32)
    row_total = jnp.ones((count, block), jnp.float32)
    for step in range(ITERS):

        def col_step(acc, item):
            tb, rb = item
            return (acc + jnp.dot(rb, expo_of(tb), precision=lax.Precision.HIGHEST, preferred_element_type=jnp.float32), None)
        col, _ = lax.scan(col_step, jnp.zeros((PROTOS,), jnp.float32), (t_blocks, row_scale))
        col_scale = 1.0 / (PROTOS * col)

        def row_step(tb):
            return jnp.dot(expo_of(tb), col_scale, precision=lax.Precision.HIGHEST, preferred_element_type=jnp.float32)
        row_total = lax.map(row_step, t_blocks)
        row_scale = 1.0 / (BATCH * row_total)
    factor = PROTOS / (BATCH * student_temp)

    def final(acc, item):
        tb, sb, rt = item
        targets = expo_of(tb) * col_scale[None, :] / rt[:, None]
        logits = by_rows(sb, s_dirs) / student_temp
        expl = jnp.exp(logits)
        totals = lax.optimization_barrier(jnp.sum(expl, axis=1))
        cross = lax.optimization_barrier(jnp.sum(targets * logits, axis=1))
        loss = jnp.log(totals) - cross
        dlog = ((expl / totals[:, None] - targets) * factor).astype(jnp.bfloat16)
        fgrad = jnp.dot(dlog, s_dirs, preferred_element_type=jnp.float32).astype(jnp.bfloat16)
        acc = acc + lax.dot_general(dlog, sb, (((0,), (0,)), ((), ())), preferred_element_type=jnp.float32)
        return (acc, (loss, fgrad))
    pgrad, outs = lax.scan(final, jnp.zeros((PROTOS, DIM), jnp.float32), (t_blocks, s_blocks, row_total))
    loss, fgrad = outs
    return (loss.reshape(BATCH), fgrad.reshape(BATCH, DIM), pgrad.astype(jnp.bfloat16))
```

```python
import jax
import jax.numpy as jnp
from jax import lax
from jax.sharding import PartitionSpec as P

ITERS = 3


teacher_temp = 0.07
student_temp = 0.1


def unit_rows(x):
    xf = x.astype(jnp.float32)
    return (xf * lax.rsqrt(jnp.sum(xf * xf, axis=1, keepdims=True) + 1e-06)).astype(jnp.bfloat16)


def by_rows(left, right):
    return lax.dot_general(
        left, right, (((1,), (1,)), ((), ())), preferred_element_type=jnp.float32
    )


def by_cols(left, right):
    return lax.dot_general(
        left, right, (((0,), (0,)), ((), ())), preferred_element_type=jnp.float32
    )


def local(teacher_feat, student_feat, teacher_protos, student_protos):
    both = ("dp", "proto")
    data_count = lax.axis_size("dp")
    mine = teacher_protos.shape[0] // data_count
    start = lax.axis_index("dp") * mine
    t_unit = lax.all_gather(unit_rows(teacher_feat), "dp", tiled=True)
    s_unit = lax.all_gather(unit_rows(student_feat), "dp", tiled=True)
    t_dirs = unit_rows(lax.dynamic_slice_in_dim(teacher_protos, start, mine, 0))
    s_dirs = unit_rows(lax.dynamic_slice_in_dim(student_protos, start, mine, 0))
    batch_total = t_unit.shape[0]
    proto_total = mine * data_count * lax.axis_size("proto")
    expo = jnp.exp(by_rows(t_unit, t_dirs) / teacher_temp)
    row_scale = jnp.ones((batch_total,), jnp.float32)
    for step in range(ITERS):
        col_scale = 1.0 / (proto_total * jnp.sum(expo * row_scale[:, None], axis=0))
        row_total = lax.psum(jnp.sum(expo * col_scale[None, :], axis=1), both)
        row_scale = 1.0 / (batch_total * row_total)
    targets = expo * col_scale[None, :] / row_total[:, None]
    logits = by_rows(s_unit, s_dirs) / student_temp
    expl = jnp.exp(logits)
    totals, cross = lax.psum((jnp.sum(expl, axis=1), jnp.sum(targets * logits, axis=1)), both)
    row_loss = jnp.log(totals) - cross
    rows_local = teacher_feat.shape[0]
    row_loss = lax.dynamic_slice_in_dim(row_loss, lax.axis_index("dp") * rows_local, rows_local, 0)
    factor = proto_total / (batch_total * student_temp)
    dlog = ((expl / totals[:, None] - targets) * factor).astype(jnp.bfloat16)
    proto_grad = by_cols(dlog, s_unit).astype(jnp.bfloat16)
    feature_terms = jnp.dot(dlog, s_dirs, preferred_element_type=jnp.float32)
    feature_grad = lax.psum_scatter(feature_terms, "dp", scatter_dimension=0, tiled=True)
    feature_grad = lax.psum(feature_grad, "proto").astype(jnp.bfloat16)
    return (row_loss, feature_grad, proto_grad)


def solution(mesh):
    placed = (P("dp", None), P("dp", None), P("proto", None), P("proto", None))
    return jax.shard_map(
        local,
        mesh=mesh,
        in_specs=placed,
        out_specs=(P("dp"), P("dp", None), P(("proto", "dp"), None)),
        check_vma=False,
    )
```

```python
import functools
import math

import jax
import jax.numpy as jnp
from jax import lax
from jax.experimental import pallas as pl
from jax.experimental.pallas import tpu as pltpu
from jax.sharding import PartitionSpec as P

ITERS = 3
teacher_temp = 0.07
student_temp = 0.1
LOG2E = math.log2(math.e)
MESH = pl.DeviceIdType.MESH
f32, bf16 = jnp.float32, jnp.bfloat16


def unit_rows(x):
    xf = x.astype(f32)
    return (xf * lax.rsqrt(jnp.sum(xf * xf, axis=1, keepdims=True) + 1e-06)).astype(bf16)


def by_rows(left, right):
    return lax.dot_general(left, right, (((1,), (1,)), ((), ())), preferred_element_type=f32)


def by_cols(left, right):
    return lax.dot_general(left, right, (((0,), (0,)), ((), ())), preferred_element_type=f32)


def split16(x):
    n = x.shape[1]
    hi = x.astype(bf16).astype(f32)
    row = lax.broadcasted_iota(jnp.int32, (16, n), 0)
    return jnp.where(row == 0, hi, jnp.where(row == 1, x - hi, 0.0)).astype(bf16)


def kernel(
    D, Q, tf, sf, tp, sp, stats, fterm, pg,
    tdir, sdir, tu, su, expo, expl, dblk, acc, colv, vec, rowp, part, b1, b2, fin,
    load_sem, gs, gr, asem, rsem,
):
    R, K = tf.shape
    M = tdir.shape[0]
    B = D * R
    NZ, PS = D // 2, 2 * Q
    C = B // PS
    per = C // R
    H = R // 2
    NC = min(M, 512)
    protos = M * D * Q
    dp, q = lax.axis_index("dp"), lax.axis_index("proto")
    z, x, c = dp // 2, lax.rem(dp, 2), lax.rem(q, 2)
    p = q + Q * x
    core = q + 1 - 2 * c

    def plane(j):
        p2 = lax.rem(p + j, PS)
        return p2, {"dp": z * 2 + p2 // Q, "proto": lax.rem(p2, Q)}

    def column(j):
        return {"dp": lax.rem(z + j, NZ) * 2 + x, "proto": q}

    loads = [
        pltpu.make_async_copy(src.at[pl.ds(pl.multiple_of(dp * M, M), M), :], dst, load_sem.at[n])
        for n, (src, dst) in enumerate(((tp, tdir), (sp, sdir)))
    ]
    for cp in loads:
        cp.start()

    barrier = pltpu.get_barrier_semaphore()
    for j in range(1, PS):
        pl.semaphore_signal(barrier, inc=1, device_id=plane(j)[1], device_id_type=MESH)
    for j in range(1, NZ):
        pl.semaphore_signal(barrier, inc=1, device_id=column(j), device_id_type=MESH)

    tu[pl.ds(pl.multiple_of(dp * R, R), R), :] = unit_rows(tf[...])
    su[pl.ds(pl.multiple_of(dp * R, R), R), :] = unit_rows(sf[...])
    pl.semaphore_wait(barrier, PS - 1 + NZ - 1)

    bufs = (tu, su)
    RIGHT, LEFT, ACROSS, OTHER = range(4)

    def half(t, d, cc):
        return bufs[t].at[pl.ds(pl.multiple_of(d * R + cc * H, H), H), :]

    def move(t, route, d):
        dev = (
            {"dp": lax.min(dp + 2, D - 2 + x), "proto": q},
            {"dp": lax.max(dp - 2, x), "proto": q},
            {"dp": z * 2 + 1 - x, "proto": q},
            {"dp": dp, "proto": core},
        )[route]
        return pltpu.make_async_remote_copy(
            src_ref=half(t, d, c), dst_ref=half(t, d, c),
            send_sem=gs.at[t, route, d], recv_sem=gr.at[t, d, c],
            device_id=dev, device_id_type=MESH,
        )

    def arrived(t, d, cc):
        pltpu.make_async_remote_copy(
            src_ref=half(t, d, cc), dst_ref=half(t, d, cc),
            send_sem=gs.at[t, 0, d], recv_sem=gr.at[t, d, cc],
            device_id={"dp": dp, "proto": core}, device_id_type=MESH,
        ).wait_recv()

    def go(t, route, d):
        move(t, route, d).start()

    def start_own(t):
        pl.when(z < NZ - 1)(lambda: go(t, RIGHT, dp))
        pl.when(z > 0)(lambda: go(t, LEFT, dp))
        go(t, ACROSS, dp)

    def along(t, s):
        @pl.when(z - s >= 0)
        def _():
            d = (z - s) * 2 + x
            arrived(t, d, c)
            pl.when(z < NZ - 1)(lambda: go(t, RIGHT, d))
            go(t, ACROSS, d)
            go(t, OTHER, d)

        @pl.when(z + s < NZ)
        def _():
            d = (z + s) * 2 + x
            arrived(t, d, c)
            pl.when(z > 0)(lambda: go(t, LEFT, d))
            go(t, ACROSS, d)
            go(t, OTHER, d)

    def across(t, s):
        @pl.when(z - s >= 0)
        def _():
            d = (z - s) * 2 + 1 - x
            arrived(t, d, c)
            go(t, OTHER, d)

        @pl.when((z + s < NZ) & (s > 0))
        def _():
            d = (z + s) * 2 + 1 - x
            arrived(t, d, c)
            go(t, OTHER, d)

    def sent(t):
        def body(d, _):
            zz, xx = d // 2, lax.rem(d, 2)

            @pl.when(xx == x)
            def _():
                pl.when((zz <= z) & (z < NZ - 1))(lambda: move(t, RIGHT, d).wait_send())
                pl.when((zz >= z) & (z > 0))(lambda: move(t, LEFT, d).wait_send())
                move(t, ACROSS, d).wait_send()

            pl.when(d != dp)(lambda: move(t, OTHER, d).wait_send())
            return 0

        lax.fori_loop(0, D, body, 0)

    start_own(0)
    start_own(1)

    def unit_dirs(ref):
        step = min(M, 512)
        for n in range(0, M, step):
            ref[n:n + step, :] = unit_rows(ref[n:n + step, :])

    loads[0].wait()
    unit_dirs(tdir)
    colv[...] = jnp.zeros_like(colv)

    def rows(i):
        return pl.ds(pl.multiple_of(i * R, R), R)

    def teach(i):
        a = tu[rows(i), :]
        for n in range(0, M, NC):
            e = jnp.exp2(by_rows(a, tdir[n:n + NC, :]) * (LOG2E / teacher_temp))
            expo[rows(i), n:n + NC] = e.astype(bf16)
            colv[:, n:n + NC] += jnp.sum(e, axis=0, keepdims=True)

    def teach_at(s):
        def body(k, _):
            zz = z + s * (2 * (k // 2) - 1)
            d = zz * 2 + lax.rem(x + lax.rem(k, 2), 2)
            ok = (zz >= 0) & (zz < NZ) & ((s > 0) | (k < 2))

            @pl.when(ok)
            def _():
                pl.when(d != dp)(lambda: arrived(0, d, 1 - c))
                teach(d)

            return 0

        lax.fori_loop(0, 4, body, 0)

    def gather_step(s, _):
        pl.when(s + 1 < NZ)(lambda: along(0, s + 1))
        across(0, s)
        teach_at(s)
        return 0

    lax.fori_loop(0, NZ, gather_step, 0)

    def place(i):
        return i // per, pl.multiple_of(lax.rem(i, per) * R, R)

    def row_pass(it):
        cs = split16(colv[...])

        def body(i, _):
            o = by_rows(cs, expo[rows(i), :])
            ci, off = place(i)
            rowp[it, ci, :, pl.ds(off, R)] = o[0:1] + o[1:2]
            return 0

        lax.fori_loop(0, D, body, 0)

    def col_pass(it):
        for i in range(D):
            off = (i % per) * R
            vec[i] = split16(1.0 / (B * fin[it, i // per, :, off:off + R]))

        def body(i, a):
            return a + jnp.dot(vec[i], expo[rows(i), :], preferred_element_type=f32)

        a = lax.fori_loop(0, D, body, jnp.zeros((16, M), f32))
        colv[...] = 1.0 / (protos * (a[0:1] + a[1:2]))

    def send(it, k, src, dst, dev):
        cp = pltpu.make_async_remote_copy(
            src_ref=src, dst_ref=dst, send_sem=asem.at[it, k], recv_sem=rsem.at[it, k],
            device_id=dev, device_id_type=MESH,
        )
        cp.start()
        return cp

    def all_reduce(it, values, first=None, second=None, third=None):
        n = values * C
        started = []
        for j in range(1, PS):
            p2, dev = plane(j)
            started.append(send(it, j - 1, rowp.at[it, p2, :, 0:n], b1.at[it, j - 1, :, 0:n], dev))
        if first is not None:
            first()
        for cp in started:
            cp.wait_recv()
        total = rowp[it, p, :, 0:n]
        for j in range(1, PS):
            total = total + b1[it, j - 1, :, 0:n]
        part[it, :, 0:n] = total
        ring = []
        for j in range(1, NZ):
            ring.append(send(it, PS - 2 + j, part.at[it, :, 0:n], b2.at[it, j - 1, :, 0:n], column(j)))
        if second is not None:
            second()
        for cp in ring:
            cp.wait_recv()
        for j in range(1, NZ):
            total = total + b2[it, j - 1, :, 0:n]
        fin[it, p, :, 0:n] = total
        last = []
        for j in range(1, PS):
            _, dev = plane(j)
            here = fin.at[it, p, :, 0:n]
            last.append(send(it, PS + NZ - 3 + j, here, here, dev))
        if third is not None:
            third()
        for j, cp in enumerate(last, 1):
            cp.wait_send()
            there = fin.at[it, lax.rem(p + PS - j, PS), :, 0:n]
            pltpu.make_async_remote_copy(
                src_ref=there, dst_ref=there, send_sem=asem.at[it, PS + NZ - 3 + j],
                recv_sem=rsem.at[it, PS + NZ - 3 + j], device_id=plane(j)[1], device_id_type=MESH,
            ).wait_recv()
        for cp in started + ring:
            cp.wait_send()

    def learn(i, _):
        pl.when(i != dp)(lambda: arrived(1, i, 1 - c))
        a = su[rows(i), :]
        ones = jnp.ones((16, NC), bf16)
        tot = jnp.zeros((16, R), f32)
        dot = jnp.zeros((16, R), f32)
        for n in range(0, M, NC):
            lg = by_rows(a, sdir[n:n + NC, :]) * (1.0 / student_temp)
            e = jnp.exp2(lg * LOG2E)
            eb = e.astype(bf16)
            expl[rows(i), n:n + NC] = eb
            tot = tot + by_rows(ones, eb)
            dot = dot + by_rows(ones, (e * lg).astype(bf16))
        ci, off = place(i)
        rowp[2, ci, :, pl.ds(off + C, R)] = tot[0:1]
        rowp[2, ci, :, pl.ds(off + 2 * C, R)] = dot[0:1]
        return 0

    def student_dirs():
        loads[1].wait()
        unit_dirs(sdir)

    def gather_rest():
        def body(s, _):
            pl.when(s + 1 < NZ)(lambda: along(1, s + 1))
            across(1, s)
            return 0

        lax.fori_loop(1, NZ, body, 0)

    def student():
        lax.fori_loop(0, D, learn, 0)

    colv[...] = 1.0 / (protos * colv[...])
    along(1, 1)
    across(1, 0)
    row_pass(0)
    all_reduce(0, 1, student_dirs, None, gather_rest)
    col_pass(0)
    row_pass(1)
    all_reduce(1, 1, student)
    col_pass(1)
    row_pass(2)
    all_reduce(2, 3)

    factor = protos / (B * student_temp)
    own, off = place(dp)
    stats[0:1, :] = fin[2, own, :, pl.ds(off + C, R)]
    stats[1:2, :] = fin[2, own, :, pl.ds(off + 2 * C, R)]
    acc[...] = jnp.zeros_like(acc)

    def grads(i, _):
        ci, off = place(i)
        rt = fin[2, ci, :, pl.ds(off, R)]
        tot = fin[2, ci, :, pl.ds(off + C, R)]
        row = lax.broadcasted_iota(jnp.int32, (8, R), 0)
        sides = jnp.where(row == 0, factor / tot, factor / rt).T
        pa, ra = sides[:, 0:1], sides[:, 1:2]
        for n in range(0, M, NC):
            e = expl[rows(i), n:n + NC].astype(f32)
            t = expo[rows(i), n:n + NC].astype(f32)
            dblk[:, n:n + NC] = (e * pa - (t * colv[:, n:n + NC]) * ra).astype(bf16)
        fterm[rows(i), :] = jnp.dot(dblk[...], sdir[...], preferred_element_type=f32)
        s = su[rows(i), :]
        for n in range(0, M, NC):
            acc[:, n:n + NC] += by_cols(s, dblk[:, n:n + NC])
        return 0

    lax.fori_loop(0, D, grads, 0)
    step = min(M, 256)
    for n in range(0, M, step):
        pg[n:n + step, :] = acc[:, n:n + step].T.astype(bf16)
    sent(0)
    sent(1)


def local(teacher_feat, student_feat, teacher_protos, student_protos):
    D, Q = lax.axis_size("dp"), lax.axis_size("proto")
    R, K = teacher_feat.shape
    M = teacher_protos.shape[0] // D
    B = D * R
    NZ, PS = D // 2, 2 * Q
    C = B // PS
    V = 3 * C
    hops = PS - 1 + NZ - 1 + PS - 1
    vmem = pl.BlockSpec(memory_space=pltpu.VMEM)
    hbm = pl.BlockSpec(memory_space=pl.ANY)
    stats, terms, proto_grad = pl.pallas_call(
        functools.partial(kernel, D, Q),
        out_shape=(
            jax.ShapeDtypeStruct((2, R), f32),
            jax.ShapeDtypeStruct((B, K), f32),
            jax.ShapeDtypeStruct((M, K), bf16),
        ),
        in_specs=[vmem, vmem, hbm, hbm],
        out_specs=(vmem, vmem, vmem),
        scratch_shapes=[
            pltpu.VMEM((M, K), bf16),
            pltpu.VMEM((M, K), bf16),
            pltpu.VMEM((B, K), bf16),
            pltpu.VMEM((B, K), bf16),
            pltpu.VMEM((B, M), bf16),
            pltpu.VMEM((B, M), bf16),
            pltpu.VMEM((R, M), bf16),
            pltpu.VMEM((K, M), f32),
            pltpu.VMEM((1, M), f32),
            pltpu.VMEM((D, 16, R), bf16),
            pltpu.VMEM((ITERS, PS, 1, V), f32),
            pltpu.VMEM((ITERS, 1, V), f32),
            pltpu.VMEM((ITERS, PS - 1, 1, V), f32),
            pltpu.VMEM((ITERS, NZ - 1, 1, V), f32),
            pltpu.VMEM((ITERS, PS, 1, V), f32),
            pltpu.SemaphoreType.DMA((2,)),
            pltpu.SemaphoreType.DMA((2, 4, D)),
            pltpu.SemaphoreType.DMA((2, D, 2)),
            pltpu.SemaphoreType.DMA((ITERS, hops)),
            pltpu.SemaphoreType.DMA((ITERS, hops)),
        ],
        compiler_params=pltpu.CompilerParams(
            collective_id=0, has_side_effects=True, vmem_limit_bytes=62 * 2**20
        ),
    )(teacher_feat, student_feat, teacher_protos, student_protos)
    factor = M * D * Q / (B * student_temp)
    grad = lax.psum_scatter(terms, "dp", scatter_dimension=0, tiled=True)
    grad = lax.psum(grad, "proto")
    unit = unit_rows(student_feat).astype(f32)
    cross = stats[1] / stats[0] - jnp.sum(unit * grad, axis=1) / (student_temp * factor)
    return jnp.log(stats[0]) - cross, grad.astype(bf16), proto_grad


def solution(mesh):
    placed = (P("dp", None), P("dp", None), P("proto", None), P("proto", None))
    return jax.shard_map(
        local,
        mesh=mesh,
        in_specs=placed,
        out_specs=(P("dp"), P("dp", None), P(("proto", "dp"), None)),
        check_vma=False,
    )
```

```python
import functools
import math

import jax
import jax.numpy as jnp
from jax import lax
from jax.experimental import pallas as pl
from jax.experimental.pallas import tpu as pltpu
from jax.sharding import PartitionSpec as P

ITERS = 3
teacher_temp = 0.07
student_temp = 0.1
LOG2E = math.log2(math.e)
MESH = pl.DeviceIdType.MESH
f32, bf16 = jnp.float32, jnp.bfloat16


def unit_rows(x):
    xf = x.astype(f32)
    return (xf * lax.rsqrt(jnp.sum(xf * xf, axis=1, keepdims=True) + 1e-06)).astype(bf16)


def by_rows(left, right):
    return lax.dot_general(left, right, (((1,), (1,)), ((), ())), preferred_element_type=f32)


def by_cols(left, right):
    return lax.dot_general(left, right, (((0,), (0,)), ((), ())), preferred_element_type=f32)


def split16(x):
    n = x.shape[1]
    hi = x.astype(bf16).astype(f32)
    row = lax.broadcasted_iota(jnp.int32, (16, n), 0)
    return jnp.where(row == 0, hi, jnp.where(row == 1, x - hi, 0.0)).astype(bf16)


def kernel(
    D, Q, tf, sf, tp, sp, stats, fg, pg,
    tdir, sdir, tu, su, expo, expl, acc, colv, vec, rowp, part, b1, b2, fin,
    terms, hold, s_c, r_c, s_xa, r_xa, s_yb, r_yb, s_ya, r_ya, s_xb, r_xb, s_z, r_z, own_z, r_g,
    load_sem, gs, gr, asem, rsem, ssend, srecv,
):
    R, K = tf.shape
    M = tdir.shape[0]
    B = D * R
    NZ, PS = D // 2, 2 * Q
    C = B // PS
    per = C // R
    H = R // 2
    NC = min(M, 512)
    protos = M * D * Q
    dp, q = lax.axis_index("dp"), lax.axis_index("proto")
    z, x, c = dp // 2, lax.rem(dp, 2), lax.rem(q, 2)
    p = q + Q * x
    core = q + 1 - 2 * c

    def plane(j):
        p2 = lax.rem(p + j, PS)
        return p2, {"dp": z * 2 + p2 // Q, "proto": lax.rem(p2, Q)}

    def column(j):
        return {"dp": lax.rem(z + j, NZ) * 2 + x, "proto": q}

    loads = [
        pltpu.make_async_copy(src.at[pl.ds(pl.multiple_of(dp * M, M), M), :], dst, load_sem.at[n])
        for n, (src, dst) in enumerate(((tp, tdir), (sp, sdir)))
    ]
    for cp in loads:
        cp.start()

    barrier = pltpu.get_barrier_semaphore()
    for j in range(1, PS):
        pl.semaphore_signal(barrier, inc=1, device_id=plane(j)[1], device_id_type=MESH)
    for j in range(1, NZ):
        pl.semaphore_signal(barrier, inc=1, device_id=column(j), device_id_type=MESH)

    tu[pl.ds(pl.multiple_of(dp * R, R), R), :] = unit_rows(tf[...])
    su[pl.ds(pl.multiple_of(dp * R, R), R), :] = unit_rows(sf[...])
    pl.semaphore_wait(barrier, PS - 1 + NZ - 1)

    bufs = (tu, su)
    RIGHT, LEFT, ACROSS, OTHER = range(4)

    def half(t, d, cc):
        return bufs[t].at[pl.ds(pl.multiple_of(d * R + cc * H, H), H), :]

    def move(t, route, d):
        dev = (
            {"dp": lax.min(dp + 2, D - 2 + x), "proto": q},
            {"dp": lax.max(dp - 2, x), "proto": q},
            {"dp": z * 2 + 1 - x, "proto": q},
            {"dp": dp, "proto": core},
        )[route]
        return pltpu.make_async_remote_copy(
            src_ref=half(t, d, c), dst_ref=half(t, d, c),
            send_sem=gs.at[t, route, d], recv_sem=gr.at[t, d, c],
            device_id=dev, device_id_type=MESH,
        )

    def arrived(t, d, cc):
        pltpu.make_async_remote_copy(
            src_ref=half(t, d, cc), dst_ref=half(t, d, cc),
            send_sem=gs.at[t, 0, d], recv_sem=gr.at[t, d, cc],
            device_id={"dp": dp, "proto": core}, device_id_type=MESH,
        ).wait_recv()

    def go(t, route, d):
        move(t, route, d).start()

    def start_own(t):
        pl.when(z < NZ - 1)(lambda: go(t, RIGHT, dp))
        pl.when(z > 0)(lambda: go(t, LEFT, dp))
        go(t, ACROSS, dp)

    def along(t, s):
        @pl.when(z - s >= 0)
        def _():
            d = (z - s) * 2 + x
            arrived(t, d, c)
            pl.when(z < NZ - 1)(lambda: go(t, RIGHT, d))
            go(t, ACROSS, d)
            go(t, OTHER, d)

        @pl.when(z + s < NZ)
        def _():
            d = (z + s) * 2 + x
            arrived(t, d, c)
            pl.when(z > 0)(lambda: go(t, LEFT, d))
            go(t, ACROSS, d)
            go(t, OTHER, d)

    def across(t, s):
        @pl.when(z - s >= 0)
        def _():
            d = (z - s) * 2 + 1 - x
            arrived(t, d, c)
            go(t, OTHER, d)

        @pl.when((z + s < NZ) & (s > 0))
        def _():
            d = (z + s) * 2 + 1 - x
            arrived(t, d, c)
            go(t, OTHER, d)

    def sent(t):
        def body(d, _):
            zz, xx = d // 2, lax.rem(d, 2)

            @pl.when(xx == x)
            def _():
                pl.when((zz <= z) & (z < NZ - 1))(lambda: move(t, RIGHT, d).wait_send())
                pl.when((zz >= z) & (z > 0))(lambda: move(t, LEFT, d).wait_send())
                move(t, ACROSS, d).wait_send()

            pl.when(d != dp)(lambda: move(t, OTHER, d).wait_send())
            return 0

        lax.fori_loop(0, D, body, 0)

    start_own(0)
    start_own(1)

    def unit_dirs(ref):
        step = min(M, 512)
        for n in range(0, M, step):
            ref[n:n + step, :] = unit_rows(ref[n:n + step, :])

    loads[0].wait()
    unit_dirs(tdir)
    colv[...] = jnp.zeros_like(colv)

    def rows(i):
        return pl.ds(pl.multiple_of(i * R, R), R)

    def teach(i):
        a = tu[rows(i), :]
        for n in range(0, M, NC):
            e = jnp.exp2(by_rows(a, tdir[n:n + NC, :]) * (LOG2E / teacher_temp))
            expo[rows(i), n:n + NC] = e.astype(bf16)
            colv[:, n:n + NC] += jnp.sum(e, axis=0, keepdims=True)

    def teach_at(s):
        def body(k, _):
            zz = z + s * (2 * (k // 2) - 1)
            d = zz * 2 + lax.rem(x + lax.rem(k, 2), 2)
            ok = (zz >= 0) & (zz < NZ) & ((s > 0) | (k < 2))

            @pl.when(ok)
            def _():
                pl.when(d != dp)(lambda: arrived(0, d, 1 - c))
                teach(d)

            return 0

        lax.fori_loop(0, 4, body, 0)

    def gather_step(s, _):
        pl.when(s + 1 < NZ)(lambda: along(0, s + 1))
        across(0, s)
        teach_at(s)
        return 0

    lax.fori_loop(0, NZ, gather_step, 0)

    def place(i):
        return i // per, pl.multiple_of(lax.rem(i, per) * R, R)

    def row_pass(it):
        cs = split16(colv[...])

        def body(i, _):
            o = by_rows(cs, expo[rows(i), :])
            ci, off = place(i)
            rowp[it, ci, :, pl.ds(off, R)] = o[0:1] + o[1:2]
            return 0

        lax.fori_loop(0, D, body, 0)

    def col_pass(it):
        for i in range(D):
            off = (i % per) * R
            vec[i] = split16(1.0 / (B * fin[it, i // per, :, off:off + R]))

        def body(i, a):
            return a + jnp.dot(vec[i], expo[rows(i), :], preferred_element_type=f32)

        a = lax.fori_loop(0, D, body, jnp.zeros((16, M), f32))
        colv[...] = 1.0 / (protos * (a[0:1] + a[1:2]))

    def send(it, k, src, dst, dev):
        cp = pltpu.make_async_remote_copy(
            src_ref=src, dst_ref=dst, send_sem=asem.at[it, k], recv_sem=rsem.at[it, k],
            device_id=dev, device_id_type=MESH,
        )
        cp.start()
        return cp

    def all_reduce(it, values, first=None, second=None, third=None):
        n = values * C
        started = []
        for j in range(1, PS):
            p2, dev = plane(j)
            started.append(send(it, j - 1, rowp.at[it, p2, :, 0:n], b1.at[it, j - 1, :, 0:n], dev))
        if first is not None:
            first()
        for cp in started:
            cp.wait_recv()
        total = rowp[it, p, :, 0:n]
        for j in range(1, PS):
            total = total + b1[it, j - 1, :, 0:n]
        part[it, :, 0:n] = total
        ring = []
        for j in range(1, NZ):
            ring.append(send(it, PS - 2 + j, part.at[it, :, 0:n], b2.at[it, j - 1, :, 0:n], column(j)))
        if second is not None:
            second()
        for cp in ring:
            cp.wait_recv()
        for j in range(1, NZ):
            total = total + b2[it, j - 1, :, 0:n]
        fin[it, p, :, 0:n] = total
        last = []
        for j in range(1, PS):
            _, dev = plane(j)
            here = fin.at[it, p, :, 0:n]
            last.append(send(it, PS + NZ - 3 + j, here, here, dev))
        if third is not None:
            third()
        for j, cp in enumerate(last, 1):
            cp.wait_send()
            there = fin.at[it, lax.rem(p + PS - j, PS), :, 0:n]
            pltpu.make_async_remote_copy(
                src_ref=there, dst_ref=there, send_sem=asem.at[it, PS + NZ - 3 + j],
                recv_sem=rsem.at[it, PS + NZ - 3 + j], device_id=plane(j)[1], device_id_type=MESH,
            ).wait_recv()
        for cp in started + ring:
            cp.wait_send()

    def learn(i, _):
        pl.when(i != dp)(lambda: arrived(1, i, 1 - c))
        a = su[rows(i), :]
        ones = jnp.ones((16, NC), bf16)
        tot = jnp.zeros((16, R), f32)
        dot = jnp.zeros((16, R), f32)
        for n in range(0, M, NC):
            lg = by_rows(a, sdir[n:n + NC, :]) * (1.0 / student_temp)
            e = jnp.exp2(lg * LOG2E)
            eb = e.astype(bf16)
            expl[rows(i), n:n + NC] = eb
            tot = tot + by_rows(ones, eb)
            dot = dot + by_rows(ones, (e * lg).astype(bf16))
        ci, off = place(i)
        rowp[2, ci, :, pl.ds(off + C, R)] = tot[0:1]
        rowp[2, ci, :, pl.ds(off + 2 * C, R)] = dot[0:1]
        return 0

    def student_dirs():
        loads[1].wait()
        unit_dirs(sdir)

    def gather_rest():
        def body(s, _):
            pl.when(s + 1 < NZ)(lambda: along(1, s + 1))
            across(1, s)
            return 0

        lax.fori_loop(1, NZ, body, 0)

    def student():
        lax.fori_loop(0, D, learn, 0)

    colv[...] = 1.0 / (protos * colv[...])
    along(1, 1)
    across(1, 0)
    row_pass(0)
    all_reduce(0, 1, student_dirs, None, gather_rest)
    col_pass(0)
    row_pass(1)
    all_reduce(1, 1, student)
    col_pass(1)
    row_pass(2)
    all_reduce(2, 3)

    factor = protos / (B * student_temp)
    own, off = place(dp)
    stats[0:1, :] = fin[2, own, :, pl.ds(off + C, R)]
    stats[1:2, :] = fin[2, own, :, pl.ds(off + 2 * C, R)]
    acc[...] = jnp.zeros_like(acc)
    NY = Q // 2
    y = q // 2
    HA = H // 2
    PA = HA // NY
    to_core = {"dp": dp, "proto": core}
    to_x = {"dp": z * 2 + 1 - x, "proto": q}
    C0, XA, YB, YA, XB, Z0, G0 = 0, D, D + NZ, D + NZ * NY, D + NZ * (2 * NY - 1), D + 2 * NZ * NY, D + NZ * (2 * NY + 1)

    def to_y(j):
        y2 = lax.rem(y + j, NY)
        return y2, {"dp": dp, "proto": y2 * 2 + c}

    def hop(k, src, dst, dev):
        return pltpu.make_async_remote_copy(
            src_ref=src, dst_ref=dst, send_sem=ssend.at[k], recv_sem=srecv.at[k],
            device_id=dev, device_id_type=MESH,
        )

    def hop_core(i):
        return hop(C0 + i, s_c.at[i], r_c.at[i], to_core)

    def hop_xa(zz):
        return hop(XA + zz, s_xa.at[zz], r_xa.at[zz], to_x)

    def hop_yb(zz, j):
        return hop(YB + zz * (NY - 1) + j - 1, s_yb.at[zz, j - 1], r_yb.at[zz, j - 1], to_y(j)[1])

    def hop_ya(zz, j):
        return hop(YA + zz * (NY - 1) + j - 1, s_ya.at[zz, j - 1], r_ya.at[zz, j - 1], to_y(j)[1])

    def hop_xb(zz):
        return hop(XB + zz, s_xb.at[zz], r_xb.at[zz], to_x)

    def hop_z(j):
        return hop(Z0 + j - 1, s_z.at[j - 1], r_z.at[j - 1], column(j))

    def hop_g(j, slot):
        return hop(G0 + j - 1, r_g.at[slot], r_g.at[slot], {"dp": dp, "proto": lax.rem(q + j, Q)})

    def grads(i):
        ci, off = place(i)
        rt = fin[2, ci, :, pl.ds(off, R)]
        tot = fin[2, ci, :, pl.ds(off + C, R)]
        row = lax.broadcasted_iota(jnp.int32, (8, R), 0)
        sides = jnp.where(row == 0, factor / tot, factor / rt).T
        pa, ra = sides[:, 0:1], sides[:, 1:2]
        total = jnp.zeros((R, K), f32)
        for n in range(0, M, NC):
            e = expl[rows(i), n:n + NC].astype(f32)
            t = expo[rows(i), n:n + NC].astype(f32)
            d = (e * pa - (t * colv[:, n:n + NC]) * ra).astype(bf16)
            expl[rows(i), n:n + NC] = d
            total = total + jnp.dot(d, sdir[n:n + NC, :], preferred_element_type=f32)
        terms[...] = total
        hold[i] = terms[pl.ds(pl.multiple_of(c * H, H), H), :]
        s_c[i] = terms[pl.ds(pl.multiple_of((1 - c) * H, H), H), :].astype(bf16)
        hop_core(i).start()

    def piece(k, base):
        return pl.ds(pl.multiple_of(base + k * PA, PA), PA)

    def stage1(zz):
        for xx in range(2):
            i = zz * 2 + xx
            hop_core(i).wait_recv()
            hold[i] = hold[i] + r_c[i].astype(f32)
        s_xa[zz] = hold[zz * 2 + 1 - x, 0:HA, :].astype(bf16)
        hop_xa(zz).start()
        for j in range(1, NY):
            y2, _ = to_y(j)
            for xx in range(2):
                s_yb[zz, j - 1, xx] = hold[zz * 2 + xx, piece(y2, HA), :].astype(bf16)
            hop_yb(zz, j).start()

    def stage2(zz):
        mine, other = zz * 2 + x, zz * 2 + 1 - x
        hop_xa(zz).wait_recv()
        hold[mine, 0:HA, :] = hold[mine, 0:HA, :] + r_xa[zz].astype(f32)
        for j in range(1, NY):
            y2, _ = to_y(j)
            s_ya[zz, j - 1] = hold[mine, piece(y2, 0), :].astype(bf16)
            hop_ya(zz, j).start()
        for j in range(1, NY):
            hop_yb(zz, j).wait_recv()
            for xx in range(2):
                at = piece(y, HA)
                hold[zz * 2 + xx, at, :] = hold[zz * 2 + xx, at, :] + r_yb[zz, j - 1, xx].astype(f32)
        s_xb[zz] = hold[other, piece(y, HA), :].astype(bf16)
        hop_xb(zz).start()

    def stage3(zz):
        mine = zz * 2 + x
        first, second = hold[mine, piece(y, 0), :], hold[mine, piece(y, HA), :]
        for j in range(1, NY):
            hop_ya(zz, j).wait_recv()
            first = first + r_ya[zz, j - 1].astype(f32)
        hop_xb(zz).wait_recv()
        second = second + r_xb[zz].astype(f32)

        @pl.when(zz == z)
        def _():
            own_z[0:PA, :] = first
            own_z[PA:2 * PA, :] = second

        for j in range(1, NZ):
            @pl.when(lax.rem(z + j, NZ) == zz)
            def _():
                s_z[j - 1, 0:PA, :] = first.astype(bf16)
                s_z[j - 1, PA:2 * PA, :] = second.astype(bf16)
                hop_z(j).start()

    def grad_step(t, _):
        grads(2 * t)
        grads(2 * t + 1)
        pl.when(t >= 1)(lambda: stage1(t - 1))
        pl.when(t >= 2)(lambda: stage2(t - 2))
        pl.when(t >= 3)(lambda: stage3(t - 3))
        return 0

    lax.fori_loop(0, NZ, grad_step, 0)

    def protos_of(k):
        def body(i, _):
            s = su[rows(i), :]
            for n in range(0, M, NC):
                acc[:, n:n + NC] += by_cols(s, expl[rows(i), n:n + NC])
            return 0

        lax.fori_loop(k * D // 4, (k + 1) * D // 4, body, 0)

    stage1(NZ - 1)
    stage2(NZ - 2)
    stage3(NZ - 3)
    protos_of(0)
    stage2(NZ - 1)
    stage3(NZ - 2)
    protos_of(1)
    stage3(NZ - 1)
    protos_of(2)
    total = own_z[...]
    for j in range(1, NZ):
        hop_z(j).wait_recv()
        total = total + r_z[j - 1].astype(f32)
    r_g[q] = total.astype(bf16)
    for j in range(1, Q):
        hop_g(j, q).start()
    protos_of(3)
    chunk = min(M, 256)
    for n in range(0, M, chunk):
        pg[n:n + chunk, :] = acc[:, n:n + chunk].T.astype(bf16)
    for j in range(1, Q):
        hop_g(j, q).wait_send()
        hop_g(j, lax.rem(q + Q - j, Q)).wait_recv()
    for k in range(Q):
        base = (k % 2) * H + (k // 2) * PA
        fg[base:base + PA, :] = r_g[k, 0:PA, :]
        fg[base + HA:base + HA + PA, :] = r_g[k, PA:2 * PA, :]

    def flushed(zz, _):
        hop_core(zz * 2).wait_send()
        hop_core(zz * 2 + 1).wait_send()
        hop_xa(zz).wait_send()
        hop_xb(zz).wait_send()
        for j in range(1, NY):
            hop_yb(zz, j).wait_send()
            hop_ya(zz, j).wait_send()
        return 0

    lax.fori_loop(0, NZ, flushed, 0)
    for j in range(1, NZ):
        hop_z(j).wait_send()
    sent(0)
    sent(1)


def local(teacher_feat, student_feat, teacher_protos, student_protos):
    D, Q = lax.axis_size("dp"), lax.axis_size("proto")
    R, K = teacher_feat.shape
    M = teacher_protos.shape[0] // D
    B = D * R
    NZ, PS = D // 2, 2 * Q
    C = B // PS
    V = 3 * C
    hops = PS - 1 + NZ - 1 + PS - 1
    vmem = pl.BlockSpec(memory_space=pltpu.VMEM)
    hbm = pl.BlockSpec(memory_space=pl.ANY)
    NY = Q // 2
    H = R // 2
    HA = H // 2
    PA = HA // NY
    waits = D + NZ * (2 * NY + 1) + Q - 1
    stats, grad, proto_grad = pl.pallas_call(
        functools.partial(kernel, D, Q),
        out_shape=(
            jax.ShapeDtypeStruct((2, R), f32),
            jax.ShapeDtypeStruct((R, K), bf16),
            jax.ShapeDtypeStruct((M, K), bf16),
        ),
        in_specs=[vmem, vmem, hbm, hbm],
        out_specs=(vmem, vmem, vmem),
        scratch_shapes=[
            pltpu.VMEM((M, K), bf16),
            pltpu.VMEM((M, K), bf16),
            pltpu.VMEM((B, K), bf16),
            pltpu.VMEM((B, K), bf16),
            pltpu.VMEM((B, M), bf16),
            pltpu.VMEM((B, M), bf16),
            pltpu.VMEM((K, M), f32),
            pltpu.VMEM((1, M), f32),
            pltpu.VMEM((D, 16, R), bf16),
            pltpu.VMEM((ITERS, PS, 1, V), f32),
            pltpu.VMEM((ITERS, 1, V), f32),
            pltpu.VMEM((ITERS, PS - 1, 1, V), f32),
            pltpu.VMEM((ITERS, NZ - 1, 1, V), f32),
            pltpu.VMEM((ITERS, PS, 1, V), f32),
            pltpu.VMEM((R, K), f32),
            pltpu.VMEM((D, H, K), f32),
            pltpu.VMEM((D, H, K), bf16),
            pltpu.VMEM((D, H, K), bf16),
            pltpu.VMEM((NZ, HA, K), bf16),
            pltpu.VMEM((NZ, HA, K), bf16),
            pltpu.VMEM((NZ, NY - 1, 2, PA, K), bf16),
            pltpu.VMEM((NZ, NY - 1, 2, PA, K), bf16),
            pltpu.VMEM((NZ, NY - 1, PA, K), bf16),
            pltpu.VMEM((NZ, NY - 1, PA, K), bf16),
            pltpu.VMEM((NZ, PA, K), bf16),
            pltpu.VMEM((NZ, PA, K), bf16),
            pltpu.VMEM((NZ - 1, 2 * PA, K), bf16),
            pltpu.VMEM((NZ - 1, 2 * PA, K), bf16),
            pltpu.VMEM((2 * PA, K), f32),
            pltpu.VMEM((Q, 2 * PA, K), bf16),
            pltpu.SemaphoreType.DMA((2,)),
            pltpu.SemaphoreType.DMA((2, 4, D)),
            pltpu.SemaphoreType.DMA((2, D, 2)),
            pltpu.SemaphoreType.DMA((ITERS, hops)),
            pltpu.SemaphoreType.DMA((ITERS, hops)),
            pltpu.SemaphoreType.DMA((waits,)),
            pltpu.SemaphoreType.DMA((waits,)),
        ],
        compiler_params=pltpu.CompilerParams(
            collective_id=0, has_side_effects=True, vmem_limit_bytes=62 * 2**20
        ),
    )(teacher_feat, student_feat, teacher_protos, student_protos)
    factor = M * D * Q / (B * student_temp)
    unit = unit_rows(student_feat).astype(f32)
    cross = stats[1] / stats[0] - jnp.sum(unit * grad.astype(f32), axis=1) / (student_temp * factor)
    return jnp.log(stats[0]) - cross, grad, proto_grad


def solution(mesh):
    placed = (P("dp", None), P("dp", None), P("proto", None), P("proto", None))
    return jax.shard_map(
        local,
        mesh=mesh,
        in_specs=placed,
        out_specs=(P("dp"), P("dp", None), P(("proto", "dp"), None)),
        check_vma=False,
    )
```

```python
import functools
import math

import jax
import jax.numpy as jnp
from jax import lax
from jax.experimental import pallas as pl
from jax.experimental.pallas import tpu as pltpu
from jax.sharding import PartitionSpec as P

ITERS = 3
teacher_temp = 0.07
student_temp = 0.1
LOG2E = math.log2(math.e)
MESH = pl.DeviceIdType.MESH
f32, bf16 = jnp.float32, jnp.bfloat16


def unit_rows(x):
    xf = x.astype(f32)
    return (xf * lax.rsqrt(jnp.sum(xf * xf, axis=1, keepdims=True) + 1e-06)).astype(bf16)


def split16(x):
    n = x.shape[1]
    hi = x.astype(bf16).astype(f32)
    row = lax.broadcasted_iota(jnp.int32, (16, n), 0)
    return jnp.where(row == 0, hi, jnp.where(row == 1, x - hi, 0.0)).astype(bf16)


def kernel(
    D, Q, tf, sf, tp, sp, stats, fg, pg,
    tdir, sdir, tdir_t, sdir_t, sum_a, sum_b, tu, su, expo, expl, acc, colv, vec, rowp, part, b1, b2, fin,
    terms, hold, r_c, s_xa, r_xa, s_yb, r_yb, s_ya, r_ya, s_xb, r_xb, s_z, r_z, own_z, r_g,
    load_sem, gs, gr, asem, rsem, ssend, srecv,
):
    R, K = tf.shape
    M = tdir.shape[0]
    B = D * R
    NZ, PS = D // 2, 2 * Q
    C = B // PS
    per = C // R
    H = R // 2
    NC = min(M, 512)
    protos = M * D * Q
    dp, q = lax.axis_index("dp"), lax.axis_index("proto")
    z, x, c = dp // 2, lax.rem(dp, 2), lax.rem(q, 2)
    p = q + Q * x
    core = q + 1 - 2 * c

    def plane(j):
        p2 = lax.rem(p + j, PS)
        return p2, {"dp": z * 2 + p2 // Q, "proto": lax.rem(p2, Q)}

    def column(j):
        return {"dp": lax.rem(z + j, NZ) * 2 + x, "proto": q}

    loads = [
        pltpu.make_async_copy(src.at[pl.ds(pl.multiple_of(dp * M, M), M), :], dst, load_sem.at[n])
        for n, (src, dst) in enumerate(((tp, tdir), (sp, sdir)))
    ]
    for cp in loads:
        cp.start()

    barrier = pltpu.get_barrier_semaphore()
    for j in range(1, PS):
        pl.semaphore_signal(barrier, inc=1, device_id=plane(j)[1], device_id_type=MESH)
    for j in range(1, NZ):
        pl.semaphore_signal(barrier, inc=1, device_id=column(j), device_id_type=MESH)

    tu[pl.ds(pl.multiple_of(dp * R, R), R), :] = unit_rows(tf[...])
    su[pl.ds(pl.multiple_of(dp * R, R), R), :] = unit_rows(sf[...])
    pl.semaphore_wait(barrier, PS - 1 + NZ - 1)

    bufs = (tu, su)
    RIGHT, LEFT, ACROSS, OTHER = range(4)

    def half(t, d, cc):
        return bufs[t].at[pl.ds(pl.multiple_of(d * R + cc * H, H), H), :]

    def move(t, route, d):
        dev = (
            {"dp": lax.min(dp + 2, D - 2 + x), "proto": q},
            {"dp": lax.max(dp - 2, x), "proto": q},
            {"dp": z * 2 + 1 - x, "proto": q},
            {"dp": dp, "proto": core},
        )[route]
        return pltpu.make_async_remote_copy(
            src_ref=half(t, d, c), dst_ref=half(t, d, c),
            send_sem=gs.at[t, route, d], recv_sem=gr.at[t, d, c],
            device_id=dev, device_id_type=MESH,
        )

    def arrived(t, d, cc):
        pltpu.make_async_remote_copy(
            src_ref=half(t, d, cc), dst_ref=half(t, d, cc),
            send_sem=gs.at[t, 0, d], recv_sem=gr.at[t, d, cc],
            device_id={"dp": dp, "proto": core}, device_id_type=MESH,
        ).wait_recv()

    def go(t, route, d):
        move(t, route, d).start()

    def start_own(t):
        pl.when(z < NZ - 1)(lambda: go(t, RIGHT, dp))
        pl.when(z > 0)(lambda: go(t, LEFT, dp))
        go(t, ACROSS, dp)

    def along(t, s):
        @pl.when(z - s >= 0)
        def _():
            d = (z - s) * 2 + x
            arrived(t, d, c)
            pl.when(z < NZ - 1)(lambda: go(t, RIGHT, d))
            go(t, ACROSS, d)
            go(t, OTHER, d)

        @pl.when(z + s < NZ)
        def _():
            d = (z + s) * 2 + x
            arrived(t, d, c)
            pl.when(z > 0)(lambda: go(t, LEFT, d))
            go(t, ACROSS, d)
            go(t, OTHER, d)

    def across(t, s):
        @pl.when(z - s >= 0)
        def _():
            d = (z - s) * 2 + 1 - x
            arrived(t, d, c)
            go(t, OTHER, d)

        @pl.when((z + s < NZ) & (s > 0))
        def _():
            d = (z + s) * 2 + 1 - x
            arrived(t, d, c)
            go(t, OTHER, d)

    def sent(t):
        def body(d, _):
            zz, xx = d // 2, lax.rem(d, 2)

            @pl.when(xx == x)
            def _():
                pl.when((zz <= z) & (z < NZ - 1))(lambda: move(t, RIGHT, d).wait_send())
                pl.when((zz >= z) & (z > 0))(lambda: move(t, LEFT, d).wait_send())
                move(t, ACROSS, d).wait_send()

            pl.when(d != dp)(lambda: move(t, OTHER, d).wait_send())
            return 0

        lax.fori_loop(0, D, body, 0)

    start_own(0)

    def unit_dirs(ref, turned):
        step = min(M, 256)
        for n in range(0, M, step):
            u = unit_rows(ref[n:n + step, :])
            ref[n:n + step, :] = u
            turned[:, n:n + step] = u.astype(f32).T.astype(bf16)

    loads[0].wait()
    unit_dirs(tdir, tdir_t)
    colv[...] = jnp.zeros_like(colv)

    def rows(i):
        return pl.ds(pl.multiple_of(i * R, R), R)

    def teach(i):
        a = tu[rows(i), :]
        for n in range(0, M, NC):
            t = jnp.dot(a, tdir_t[:, n:n + NC], preferred_element_type=f32)
            e = jnp.exp2(t * (LOG2E / teacher_temp))
            expo[rows(i), n:n + NC] = e.astype(bf16)
            colv[:, n:n + NC] += jnp.sum(e, axis=0, keepdims=True)

    def teach_at(s):
        def body(k, _):
            zz = z + s * (2 * (k // 2) - 1)
            d = zz * 2 + lax.rem(x + lax.rem(k, 2), 2)
            ok = (zz >= 0) & (zz < NZ) & ((s > 0) | (k < 2))

            @pl.when(ok)
            def _():
                pl.when(d != dp)(lambda: arrived(0, d, 1 - c))
                teach(d)

            return 0

        lax.fori_loop(0, 4, body, 0)

    def gather_step(s, _):
        pl.when(s + 1 < NZ)(lambda: along(0, s + 1))
        across(0, s)
        pl.when(s == 1)(lambda: start_own(1))
        teach_at(s)
        return 0

    lax.fori_loop(0, NZ, gather_step, 0)

    def place(i):
        return i // per, pl.multiple_of(lax.rem(i, per) * R, R)

    def lanes_to_row(ref):
        return jnp.sum(ref[...].T, axis=0, keepdims=True)

    def row_pass(it):
        def body(i, _):
            for r in range(0, R, 128):
                at = pl.ds(pl.multiple_of(i * R + r, 128), 128)
                total = jnp.zeros((128, 128), f32)
                for n in range(0, M, 128):
                    total = total + expo[at, n:n + 128].astype(f32) * colv[:, n:n + 128]
                sum_a[r:r + 128, :] = total
            ci, off = place(i)
            rowp[it, ci, :, pl.ds(off, R)] = lanes_to_row(sum_a)
            return 0

        lax.fori_loop(0, D, body, 0)

    def col_pass(it):
        for i in range(D):
            off = (i % per) * R
            vec[i] = split16(1.0 / (B * fin[it, i // per, :, off:off + R]))

        def body(i, a):
            return a + jnp.dot(vec[i], expo[rows(i), :], preferred_element_type=f32)

        a = lax.fori_loop(0, D, body, jnp.zeros((16, M), f32))
        colv[...] = 1.0 / (protos * (a[0:1] + a[1:2]))

    def send(it, k, src, dst, dev):
        cp = pltpu.make_async_remote_copy(
            src_ref=src, dst_ref=dst, send_sem=asem.at[it, k], recv_sem=rsem.at[it, k],
            device_id=dev, device_id_type=MESH,
        )
        cp.start()
        return cp

    def all_reduce(it, values, first=None, second=None, third=None):
        n = values * C
        started = []
        for j in range(1, PS):
            p2, dev = plane(j)
            started.append(send(it, j - 1, rowp.at[it, p2, :, 0:n], b1.at[it, j - 1, :, 0:n], dev))
        if first is not None:
            first()
        for cp in started:
            cp.wait_recv()
        total = rowp[it, p, :, 0:n]
        for j in range(1, PS):
            total = total + b1[it, j - 1, :, 0:n]
        part[it, :, 0:n] = total
        ring = []
        for j in range(1, NZ):
            ring.append(send(it, PS - 2 + j, part.at[it, :, 0:n], b2.at[it, j - 1, :, 0:n], column(j)))
        if second is not None:
            second()
        for cp in ring:
            cp.wait_recv()
        for j in range(1, NZ):
            total = total + b2[it, j - 1, :, 0:n]
        fin[it, p, :, 0:n] = total
        last = []
        for j in range(1, PS):
            _, dev = plane(j)
            here = fin.at[it, p, :, 0:n]
            last.append(send(it, PS + NZ - 3 + j, here, here, dev))
        if third is not None:
            third()
        for j, cp in enumerate(last, 1):
            cp.wait_send()
            there = fin.at[it, lax.rem(p + PS - j, PS), :, 0:n]
            pltpu.make_async_remote_copy(
                src_ref=there, dst_ref=there, send_sem=asem.at[it, PS + NZ - 3 + j],
                recv_sem=rsem.at[it, PS + NZ - 3 + j], device_id=plane(j)[1], device_id_type=MESH,
            ).wait_recv()
        for cp in started + ring:
            cp.wait_send()

    def learn(i, _):
        pl.when(i != dp)(lambda: arrived(1, i, 1 - c))
        a = su[rows(i), :]
        for n in range(0, M, NC):
            t = jnp.dot(a, sdir_t[:, n:n + NC], preferred_element_type=f32)
            e = jnp.exp2(t * (LOG2E / student_temp))
            expl[rows(i), n:n + NC] = e.astype(bf16)
            w = e * t
            ea, wa = e[:, 0:128], w[:, 0:128]
            for k in range(128, NC, 128):
                ea, wa = ea + e[:, k:k + 128], wa + w[:, k:k + 128]
            sum_a[...] = ea if n == 0 else sum_a[...] + ea
            sum_b[...] = wa if n == 0 else sum_b[...] + wa
        ci, off = place(i)
        rowp[2, ci, :, pl.ds(off + C, R)] = lanes_to_row(sum_a)
        rowp[2, ci, :, pl.ds(off + 2 * C, R)] = lanes_to_row(sum_b) * (1.0 / student_temp)
        return 0

    def student_dirs():
        along(1, 1)
        across(1, 0)
        loads[1].wait()
        unit_dirs(sdir, sdir_t)

    def gather_rest():
        def body(s, _):
            pl.when(s + 1 < NZ)(lambda: along(1, s + 1))
            across(1, s)
            return 0

        lax.fori_loop(1, NZ, body, 0)

    def student(k):
        return lambda: lax.fori_loop(k * D // 3, (k + 1) * D // 3, learn, 0)

    colv[...] = 1.0 / (protos * colv[...])
    row_pass(0)
    all_reduce(0, 1, student_dirs, None, gather_rest)
    col_pass(0)
    row_pass(1)
    all_reduce(1, 1, student(0), student(1), student(2))
    col_pass(1)
    row_pass(2)
    all_reduce(2, 3, lambda: sent(0))

    factor = protos / (B * student_temp)
    own, off = place(dp)
    stats[0:1, :] = fin[2, own, :, pl.ds(off + C, R)]
    stats[1:2, :] = fin[2, own, :, pl.ds(off + 2 * C, R)]
    acc[...] = jnp.zeros_like(acc)
    NY = Q // 2
    y = q // 2
    HA = H // 2
    PA = HA // NY
    to_core = {"dp": dp, "proto": core}
    to_x = {"dp": z * 2 + 1 - x, "proto": q}
    C0, XA, YB, YA, XB, Z0, G0 = 0, D, D + NZ, D + NZ * NY, D + NZ * (2 * NY - 1), D + 2 * NZ * NY, D + NZ * (2 * NY + 1)

    def to_y(j):
        y2 = lax.rem(y + j, NY)
        return y2, {"dp": dp, "proto": y2 * 2 + c}

    def hop(k, src, dst, dev):
        return pltpu.make_async_remote_copy(
            src_ref=src, dst_ref=dst, send_sem=ssend.at[k], recv_sem=srecv.at[k],
            device_id=dev, device_id_type=MESH,
        )

    def hop_core(i):
        return hop(C0 + i, half(0, i, 0), r_c.at[i], to_core)

    def hop_xa(zz):
        return hop(XA + zz, s_xa.at[zz], r_xa.at[zz], to_x)

    def hop_yb(zz, j):
        return hop(YB + zz * (NY - 1) + j - 1, s_yb.at[zz, j - 1], r_yb.at[zz, j - 1], to_y(j)[1])

    def hop_ya(zz, j):
        return hop(YA + zz * (NY - 1) + j - 1, s_ya.at[zz, j - 1], r_ya.at[zz, j - 1], to_y(j)[1])

    def hop_xb(zz):
        return hop(XB + zz, s_xb.at[zz], r_xb.at[zz], to_x)

    def hop_z(j):
        return hop(Z0 + j - 1, s_z.at[j - 1], r_z.at[j - 1], column(j))

    def hop_g(j, slot):
        return hop(G0 + j - 1, r_g.at[slot], r_g.at[slot], {"dp": dp, "proto": lax.rem(q + j, Q)})

    def grads(i):
        ci, off = place(i)
        rt = fin[2, ci, :, pl.ds(off, R)]
        tot = fin[2, ci, :, pl.ds(off + C, R)]
        row = lax.broadcasted_iota(jnp.int32, (8, R), 0)
        sides = jnp.where(row == 0, factor / tot, factor / rt).T
        pa, ra = sides[:, 0:1], sides[:, 1:2]
        total = jnp.zeros((R, K), f32)
        for n in range(0, M, NC):
            e = expl[rows(i), n:n + NC].astype(f32)
            t = expo[rows(i), n:n + NC].astype(f32)
            d = (e * pa - (t * colv[:, n:n + NC]) * ra).astype(bf16)
            expl[rows(i), n:n + NC] = d
            total = total + jnp.dot(d, sdir[n:n + NC, :], preferred_element_type=f32)
        terms[...] = total
        hold[i] = terms[pl.ds(pl.multiple_of(c * H, H), H), :]
        tu[pl.ds(pl.multiple_of(i * R, R), H), :] = terms[pl.ds(pl.multiple_of((1 - c) * H, H), H), :].astype(bf16)
        hop_core(i).start()

    def piece(k, base):
        return pl.ds(pl.multiple_of(base + k * PA, PA), PA)

    def stage1(zz):
        for xx in range(2):
            i = zz * 2 + xx
            hop_core(i).wait_recv()
            hold[i] = hold[i] + r_c[i].astype(f32)
        s_xa[zz] = hold[zz * 2 + 1 - x, 0:HA, :].astype(bf16)
        hop_xa(zz).start()
        for j in range(1, NY):
            y2, _ = to_y(j)
            for xx in range(2):
                s_yb[zz, j - 1, xx] = hold[zz * 2 + xx, piece(y2, HA), :].astype(bf16)
            hop_yb(zz, j).start()

    def stage2(zz):
        mine, other = zz * 2 + x, zz * 2 + 1 - x
        hop_xa(zz).wait_recv()
        hold[mine, 0:HA, :] = hold[mine, 0:HA, :] + r_xa[zz].astype(f32)
        for j in range(1, NY):
            y2, _ = to_y(j)
            s_ya[zz, j - 1] = hold[mine, piece(y2, 0), :].astype(bf16)
            hop_ya(zz, j).start()
        for j in range(1, NY):
            hop_yb(zz, j).wait_recv()
            for xx in range(2):
                at = piece(y, HA)
                hold[zz * 2 + xx, at, :] = hold[zz * 2 + xx, at, :] + r_yb[zz, j - 1, xx].astype(f32)
        s_xb[zz] = hold[other, piece(y, HA), :].astype(bf16)
        hop_xb(zz).start()

    def stage3(zz):
        mine = zz * 2 + x
        first, second = hold[mine, piece(y, 0), :], hold[mine, piece(y, HA), :]
        for j in range(1, NY):
            hop_ya(zz, j).wait_recv()
            first = first + r_ya[zz, j - 1].astype(f32)
        hop_xb(zz).wait_recv()
        second = second + r_xb[zz].astype(f32)

        @pl.when(zz == z)
        def _():
            own_z[0:PA, :] = first
            own_z[PA:2 * PA, :] = second

        for j in range(1, NZ):
            @pl.when(lax.rem(z + j, NZ) == zz)
            def _():
                s_z[j - 1, 0:PA, :] = first.astype(bf16)
                s_z[j - 1, PA:2 * PA, :] = second.astype(bf16)
                hop_z(j).start()

    def grad_step(t, _):
        grads(2 * t)
        grads(2 * t + 1)
        pl.when(t >= 1)(lambda: stage1(t - 1))
        pl.when(t >= 2)(lambda: stage2(t - 2))
        pl.when(t >= 3)(lambda: stage3(t - 3))
        return 0

    lax.fori_loop(0, NZ, grad_step, 0)

    def protos_of(k):
        def body(i, _):
            s = su[rows(i), :].astype(f32).T.astype(bf16)
            for n in range(0, M, NC):
                acc[:, n:n + NC] += jnp.dot(s, expl[rows(i), n:n + NC], preferred_element_type=f32)
            return 0

        lax.fori_loop(k * D // 4, (k + 1) * D // 4, body, 0)

    stage1(NZ - 1)
    stage2(NZ - 2)
    stage3(NZ - 3)
    protos_of(0)
    stage2(NZ - 1)
    stage3(NZ - 2)
    protos_of(1)
    stage3(NZ - 1)
    protos_of(2)
    total = own_z[...]
    for j in range(1, NZ):
        hop_z(j).wait_recv()
        total = total + r_z[j - 1].astype(f32)
    r_g[q] = total.astype(bf16)
    for j in range(1, Q):
        hop_g(j, q).start()
    protos_of(3)
    chunk = min(M, 256)
    for n in range(0, M, chunk):
        pg[n:n + chunk, :] = acc[:, n:n + chunk].T.astype(bf16)
    for j in range(1, Q):
        hop_g(j, q).wait_send()
        hop_g(j, lax.rem(q + Q - j, Q)).wait_recv()
    for k in range(Q):
        base = (k % 2) * H + (k // 2) * PA
        fg[base:base + PA, :] = r_g[k, 0:PA, :]
        fg[base + HA:base + HA + PA, :] = r_g[k, PA:2 * PA, :]

    def flushed(zz, _):
        hop_core(zz * 2).wait_send()
        hop_core(zz * 2 + 1).wait_send()
        hop_xa(zz).wait_send()
        hop_xb(zz).wait_send()
        for j in range(1, NY):
            hop_yb(zz, j).wait_send()
            hop_ya(zz, j).wait_send()
        return 0

    lax.fori_loop(0, NZ, flushed, 0)
    for j in range(1, NZ):
        hop_z(j).wait_send()
    sent(1)


def local(teacher_feat, student_feat, teacher_protos, student_protos):
    D, Q = lax.axis_size("dp"), lax.axis_size("proto")
    R, K = teacher_feat.shape
    M = teacher_protos.shape[0] // D
    B = D * R
    NZ, PS = D // 2, 2 * Q
    C = B // PS
    V = 3 * C
    hops = PS - 1 + NZ - 1 + PS - 1
    vmem = pl.BlockSpec(memory_space=pltpu.VMEM)
    hbm = pl.BlockSpec(memory_space=pl.ANY)
    NY = Q // 2
    H = R // 2
    HA = H // 2
    PA = HA // NY
    waits = D + NZ * (2 * NY + 1) + Q - 1
    stats, grad, proto_grad = pl.pallas_call(
        functools.partial(kernel, D, Q),
        out_shape=(
            jax.ShapeDtypeStruct((2, R), f32),
            jax.ShapeDtypeStruct((R, K), bf16),
            jax.ShapeDtypeStruct((M, K), bf16),
        ),
        in_specs=[vmem, vmem, hbm, hbm],
        out_specs=(vmem, vmem, vmem),
        scratch_shapes=[
            pltpu.VMEM((M, K), bf16),
            pltpu.VMEM((M, K), bf16),
            pltpu.VMEM((K, M), bf16),
            pltpu.VMEM((K, M), bf16),
            pltpu.VMEM((R, 128), f32),
            pltpu.VMEM((R, 128), f32),
            pltpu.VMEM((B, K), bf16),
            pltpu.VMEM((B, K), bf16),
            pltpu.VMEM((B, M), bf16),
            pltpu.VMEM((B, M), bf16),
            pltpu.VMEM((K, M), f32),
            pltpu.VMEM((1, M), f32),
            pltpu.VMEM((D, 16, R), bf16),
            pltpu.VMEM((ITERS, PS, 1, V), f32),
            pltpu.VMEM((ITERS, 1, V), f32),
            pltpu.VMEM((ITERS, PS - 1, 1, V), f32),
            pltpu.VMEM((ITERS, NZ - 1, 1, V), f32),
            pltpu.VMEM((ITERS, PS, 1, V), f32),
            pltpu.VMEM((R, K), f32),
            pltpu.VMEM((D, H, K), f32),
            pltpu.VMEM((D, H, K), bf16),
            pltpu.VMEM((NZ, HA, K), bf16),
            pltpu.VMEM((NZ, HA, K), bf16),
            pltpu.VMEM((NZ, NY - 1, 2, PA, K), bf16),
            pltpu.VMEM((NZ, NY - 1, 2, PA, K), bf16),
            pltpu.VMEM((NZ, NY - 1, PA, K), bf16),
            pltpu.VMEM((NZ, NY - 1, PA, K), bf16),
            pltpu.VMEM((NZ, PA, K), bf16),
            pltpu.VMEM((NZ, PA, K), bf16),
            pltpu.VMEM((NZ - 1, 2 * PA, K), bf16),
            pltpu.VMEM((NZ - 1, 2 * PA, K), bf16),
            pltpu.VMEM((2 * PA, K), f32),
            pltpu.VMEM((Q, 2 * PA, K), bf16),
            pltpu.SemaphoreType.DMA((2,)),
            pltpu.SemaphoreType.DMA((2, 4, D)),
            pltpu.SemaphoreType.DMA((2, D, 2)),
            pltpu.SemaphoreType.DMA((ITERS, hops)),
            pltpu.SemaphoreType.DMA((ITERS, hops)),
            pltpu.SemaphoreType.DMA((waits,)),
            pltpu.SemaphoreType.DMA((waits,)),
        ],
        compiler_params=pltpu.CompilerParams(
            collective_id=0, has_side_effects=True, vmem_limit_bytes=62 * 2**20
        ),
    )(teacher_feat, student_feat, teacher_protos, student_protos)
    factor = M * D * Q / (B * student_temp)
    unit = unit_rows(student_feat).astype(f32)
    cross = stats[1] / stats[0] - jnp.sum(unit * grad.astype(f32), axis=1) / (student_temp * factor)
    return jnp.log(stats[0]) - cross, grad, proto_grad


def solution(mesh):
    placed = (P("dp", None), P("dp", None), P("proto", None), P("proto", None))
    return jax.shard_map(
        local,
        mesh=mesh,
        in_specs=placed,
        out_specs=(P("dp"), P("dp", None), P(("proto", "dp"), None)),
        check_vma=False,
    )
```

```python
import functools
import math

import jax
import jax.numpy as jnp
from jax import lax
from jax.experimental import pallas as pl
from jax.experimental.pallas import tpu as pltpu
from jax.sharding import PartitionSpec as P

ITERS = 3
teacher_temp = 0.07
student_temp = 0.1
LOG2E = math.log2(math.e)
MESH = pl.DeviceIdType.MESH
f32, bf16 = jnp.float32, jnp.bfloat16


def unit_rows(x):
    xf = x.astype(f32)
    return (xf * lax.rsqrt(jnp.sum(xf * xf, axis=1, keepdims=True) + 1e-06)).astype(bf16)


def kernel(
    D, Q, tf, sf, tp, sp, loss, fg, pg,
    tdir, sdir, tdir_t, sdir_t, sum_a, sum_b, tu, su, expo, expl, acc, colv, rowp, part, b1, b2, fin,
    terms, hold, r_c, s_xa, r_xa, s_yb, r_yb, s_ya, r_ya, s_xb, r_xb, s_z, r_z, own_z, r_g,
    load_sem, gs, gr, asem, rsem, ssend, srecv,
):
    R, K = tf.shape
    M = tdir.shape[0]
    B = D * R
    NZ, PS = D // 2, 2 * Q
    C = B // PS
    per = C // R
    H = R // 2
    NC = min(M, 512)
    protos = M * D * Q
    dp, q = lax.axis_index("dp"), lax.axis_index("proto")
    z, x, c = dp // 2, lax.rem(dp, 2), lax.rem(q, 2)
    p = q + Q * x
    core = q + 1 - 2 * c

    def plane(j):
        p2 = lax.rem(p + j, PS)
        return p2, {"dp": z * 2 + p2 // Q, "proto": lax.rem(p2, Q)}

    def column(j):
        return {"dp": lax.rem(z + j, NZ) * 2 + x, "proto": q}

    loads = [
        pltpu.make_async_copy(src.at[pl.ds(pl.multiple_of(dp * M, M), M), :], dst, load_sem.at[n])
        for n, (src, dst) in enumerate(((tp, tdir), (sp, sdir)))
    ]
    for cp in loads:
        cp.start()

    barrier = pltpu.get_barrier_semaphore()
    for j in range(1, PS):
        pl.semaphore_signal(barrier, inc=1, device_id=plane(j)[1], device_id_type=MESH)
    for j in range(1, NZ):
        pl.semaphore_signal(barrier, inc=1, device_id=column(j), device_id_type=MESH)

    tu[pl.ds(pl.multiple_of(dp * R, R), R), :] = unit_rows(tf[...])
    su[pl.ds(pl.multiple_of(dp * R, R), R), :] = unit_rows(sf[...])
    pl.semaphore_wait(barrier, PS - 1 + NZ - 1)

    bufs = (tu, su)
    RIGHT, LEFT, ACROSS, OTHER = range(4)

    def half(t, d, cc):
        return bufs[t].at[pl.ds(pl.multiple_of(d * R + cc * H, H), H), :]

    def move(t, route, d):
        dev = (
            {"dp": lax.min(dp + 2, D - 2 + x), "proto": q},
            {"dp": lax.max(dp - 2, x), "proto": q},
            {"dp": z * 2 + 1 - x, "proto": q},
            {"dp": dp, "proto": core},
        )[route]
        return pltpu.make_async_remote_copy(
            src_ref=half(t, d, c), dst_ref=half(t, d, c),
            send_sem=gs.at[t, route, d], recv_sem=gr.at[t, d, c],
            device_id=dev, device_id_type=MESH,
        )

    def arrived(t, d, cc):
        pltpu.make_async_remote_copy(
            src_ref=half(t, d, cc), dst_ref=half(t, d, cc),
            send_sem=gs.at[t, 0, d], recv_sem=gr.at[t, d, cc],
            device_id={"dp": dp, "proto": core}, device_id_type=MESH,
        ).wait_recv()

    def go(t, route, d):
        move(t, route, d).start()

    def start_own(t):
        pl.when(z < NZ - 1)(lambda: go(t, RIGHT, dp))
        pl.when(z > 0)(lambda: go(t, LEFT, dp))
        go(t, ACROSS, dp)

    def along(t, s):
        @pl.when(z - s >= 0)
        def _():
            d = (z - s) * 2 + x
            arrived(t, d, c)
            pl.when(z < NZ - 1)(lambda: go(t, RIGHT, d))
            go(t, ACROSS, d)
            go(t, OTHER, d)

        @pl.when(z + s < NZ)
        def _():
            d = (z + s) * 2 + x
            arrived(t, d, c)
            pl.when(z > 0)(lambda: go(t, LEFT, d))
            go(t, ACROSS, d)
            go(t, OTHER, d)

    def across(t, s):
        @pl.when(z - s >= 0)
        def _():
            d = (z - s) * 2 + 1 - x
            arrived(t, d, c)
            go(t, OTHER, d)

        @pl.when((z + s < NZ) & (s > 0))
        def _():
            d = (z + s) * 2 + 1 - x
            arrived(t, d, c)
            go(t, OTHER, d)

    def sent(t):
        def body(d, _):
            zz, xx = d // 2, lax.rem(d, 2)

            @pl.when(xx == x)
            def _():
                pl.when((zz <= z) & (z < NZ - 1))(lambda: move(t, RIGHT, d).wait_send())
                pl.when((zz >= z) & (z > 0))(lambda: move(t, LEFT, d).wait_send())
                move(t, ACROSS, d).wait_send()

            pl.when(d != dp)(lambda: move(t, OTHER, d).wait_send())
            return 0

        lax.fori_loop(0, D, body, 0)

    start_own(0)

    def unit_dirs(ref, turned):
        step = min(M, 256)
        for n in range(0, M, step):
            u = unit_rows(ref[n:n + step, :])
            ref[n:n + step, :] = u
            turned[:, n:n + step] = u.astype(f32).T.astype(bf16)

    loads[0].wait()
    unit_dirs(tdir, tdir_t)
    colv[...] = jnp.zeros_like(colv)

    def rows(i):
        return pl.ds(pl.multiple_of(i * R, R), R)

    def teach(i):
        a = tu[rows(i), :]
        for n in range(0, M, NC):
            t = jnp.dot(a, tdir_t[:, n:n + NC], preferred_element_type=f32)
            e = jnp.exp2(t * (LOG2E / teacher_temp))
            expo[rows(i), n:n + NC] = e.astype(bf16)
            colv[:, n:n + NC] += jnp.sum(e, axis=0, keepdims=True)

    def teach_at(s):
        def body(k, _):
            zz = z + s * (2 * (k // 2) - 1)
            d = zz * 2 + lax.rem(x + lax.rem(k, 2), 2)
            ok = (zz >= 0) & (zz < NZ) & ((s > 0) | (k < 2))

            @pl.when(ok)
            def _():
                pl.when(d != dp)(lambda: arrived(0, d, 1 - c))
                teach(d)

            return 0

        lax.fori_loop(0, 4, body, 0)

    def gather_step(s, _):
        pl.when(s + 1 < NZ)(lambda: along(0, s + 1))
        across(0, s)
        pl.when(s == 1)(lambda: start_own(1))
        teach_at(s)
        return 0

    lax.fori_loop(0, NZ, gather_step, 0)

    def place(i):
        return i // per, pl.multiple_of(lax.rem(i, per) * R, R)

    def lanes_to_row(ref):
        return jnp.sum(ref[...].T, axis=0, keepdims=True)

    def row_pass(it):
        def body(i, _):
            for r in range(0, R, 128):
                at = pl.ds(pl.multiple_of(i * R + r, 128), 128)
                total = jnp.zeros((128, 128), f32)
                for n in range(0, M, 128):
                    total = total + expo[at, n:n + 128].astype(f32) * colv[:, n:n + 128]
                sum_a[r:r + 128, :] = total
            ci, off = place(i)
            rowp[it, ci, :, pl.ds(off, R)] = lanes_to_row(sum_a)
            return 0

        lax.fori_loop(0, D, body, 0)

    def col_pass(it):
        colv[...] = jnp.zeros_like(colv)

        def body(i, _):
            ci, off = place(i)
            scale = 1.0 / (B * fin[it, ci, :, pl.ds(off, R)])
            sum_a[...] = jnp.broadcast_to(jnp.broadcast_to(scale, (8, R)).T[:, 0:1], (R, 128))
            for n in range(0, M, 128):
                total = jnp.zeros((8, 128), f32)
                for r in range(0, R, 128):
                    at = pl.ds(pl.multiple_of(i * R + r, 128), 128)
                    w = expo[at, n:n + 128].astype(f32) * sum_a[r:r + 128, :]
                    total = total + jnp.sum(w.reshape(16, 8, 128), axis=0)
                colv[:, n:n + 128] += jnp.sum(total, axis=0, keepdims=True)
            return 0

        lax.fori_loop(0, D, body, 0)
        colv[...] = 1.0 / (protos * colv[...])

    def send(it, k, src, dst, dev):
        cp = pltpu.make_async_remote_copy(
            src_ref=src, dst_ref=dst, send_sem=asem.at[it, k], recv_sem=rsem.at[it, k],
            device_id=dev, device_id_type=MESH,
        )
        cp.start()
        return cp

    def all_reduce(it, values, first=None, second=None, third=None):
        n = values * C
        started = []
        for j in range(1, PS):
            p2, dev = plane(j)
            started.append(send(it, j - 1, rowp.at[it, p2, :, 0:n], b1.at[it, j - 1, :, 0:n], dev))
        if first is not None:
            first()
        for cp in started:
            cp.wait_recv()
        total = rowp[it, p, :, 0:n]
        for j in range(1, PS):
            total = total + b1[it, j - 1, :, 0:n]
        part[it, :, 0:n] = total
        ring = []
        for j in range(1, NZ):
            ring.append(send(it, PS - 2 + j, part.at[it, :, 0:n], b2.at[it, j - 1, :, 0:n], column(j)))
        if second is not None:
            second()
        for cp in ring:
            cp.wait_recv()
        for j in range(1, NZ):
            total = total + b2[it, j - 1, :, 0:n]
        fin[it, p, :, 0:n] = total
        last = []
        for j in range(1, PS):
            _, dev = plane(j)
            here = fin.at[it, p, :, 0:n]
            last.append(send(it, PS + NZ - 3 + j, here, here, dev))
        if third is not None:
            third()
        for j, cp in enumerate(last, 1):
            cp.wait_send()
            there = fin.at[it, lax.rem(p + PS - j, PS), :, 0:n]
            pltpu.make_async_remote_copy(
                src_ref=there, dst_ref=there, send_sem=asem.at[it, PS + NZ - 3 + j],
                recv_sem=rsem.at[it, PS + NZ - 3 + j], device_id=plane(j)[1], device_id_type=MESH,
            ).wait_recv()
        for cp in started + ring:
            cp.wait_send()

    def learn(i, _):
        pl.when(i != dp)(lambda: arrived(1, i, 1 - c))
        a = su[rows(i), :]
        for n in range(0, M, NC):
            t = jnp.dot(a, sdir_t[:, n:n + NC], preferred_element_type=f32)
            e = jnp.exp2(t * (LOG2E / student_temp))
            expl[rows(i), n:n + NC] = e.astype(bf16)
            w = e * t
            ea, wa = e[:, 0:128], w[:, 0:128]
            for k in range(128, NC, 128):
                ea, wa = ea + e[:, k:k + 128], wa + w[:, k:k + 128]
            sum_a[...] = ea if n == 0 else sum_a[...] + ea
            sum_b[...] = wa if n == 0 else sum_b[...] + wa
        ci, off = place(i)
        rowp[2, ci, :, pl.ds(off + C, R)] = lanes_to_row(sum_a)
        rowp[2, ci, :, pl.ds(off + 2 * C, R)] = lanes_to_row(sum_b) * (1.0 / student_temp)
        return 0

    def student_dirs():
        along(1, 1)
        across(1, 0)
        loads[1].wait()
        unit_dirs(sdir, sdir_t)

    def gather_rest():
        def body(s, _):
            pl.when(s + 1 < NZ)(lambda: along(1, s + 1))
            across(1, s)
            return 0

        lax.fori_loop(1, NZ, body, 0)

    def student(k):
        return lambda: lax.fori_loop(k * D // 3, (k + 1) * D // 3, learn, 0)

    colv[...] = 1.0 / (protos * colv[...])
    row_pass(0)
    all_reduce(0, 1, student_dirs, None, gather_rest)
    col_pass(0)
    row_pass(1)
    all_reduce(1, 1, student(0), student(1), student(2))
    col_pass(1)
    row_pass(2)
    all_reduce(2, 3, lambda: sent(0))

    factor = protos / (B * student_temp)
    acc[...] = jnp.zeros_like(acc)
    NY = Q // 2
    y = q // 2
    HA = H // 2
    PA = HA // NY
    to_core = {"dp": dp, "proto": core}
    to_x = {"dp": z * 2 + 1 - x, "proto": q}
    C0, XA, YB, YA, XB, Z0, G0 = 0, D, D + NZ, D + NZ * NY, D + NZ * (2 * NY - 1), D + 2 * NZ * NY, D + NZ * (2 * NY + 1)

    def to_y(j):
        y2 = lax.rem(y + j, NY)
        return y2, {"dp": dp, "proto": y2 * 2 + c}

    def hop(k, src, dst, dev):
        return pltpu.make_async_remote_copy(
            src_ref=src, dst_ref=dst, send_sem=ssend.at[k], recv_sem=srecv.at[k],
            device_id=dev, device_id_type=MESH,
        )

    def hop_core(i):
        return hop(C0 + i, half(0, i, 0), r_c.at[i], to_core)

    def hop_xa(zz):
        return hop(XA + zz, s_xa.at[zz], r_xa.at[zz], to_x)

    def hop_yb(zz, j):
        return hop(YB + zz * (NY - 1) + j - 1, s_yb.at[zz, j - 1], r_yb.at[zz, j - 1], to_y(j)[1])

    def hop_ya(zz, j):
        return hop(YA + zz * (NY - 1) + j - 1, s_ya.at[zz, j - 1], r_ya.at[zz, j - 1], to_y(j)[1])

    def hop_xb(zz):
        return hop(XB + zz, s_xb.at[zz], r_xb.at[zz], to_x)

    def hop_z(j):
        return hop(Z0 + j - 1, s_z.at[j - 1], r_z.at[j - 1], column(j))

    def hop_g(j, slot):
        return hop(G0 + j - 1, r_g.at[slot], r_g.at[slot], {"dp": dp, "proto": lax.rem(q + j, Q)})

    def grads(i):
        ci, off = place(i)
        rt = fin[2, ci, :, pl.ds(off, R)]
        tot = fin[2, ci, :, pl.ds(off + C, R)]
        row = lax.broadcasted_iota(jnp.int32, (8, R), 0)
        sides = jnp.where(row == 0, factor / tot, factor / rt).T
        pa, ra = sides[:, 0:1], sides[:, 1:2]
        total = jnp.zeros((R, K), f32)
        for n in range(0, M, NC):
            e = expl[rows(i), n:n + NC].astype(f32)
            t = expo[rows(i), n:n + NC].astype(f32)
            d = (e * pa - (t * colv[:, n:n + NC]) * ra).astype(bf16)
            expl[rows(i), n:n + NC] = d
            total = total + jnp.dot(d, sdir[n:n + NC, :], preferred_element_type=f32)
        terms[...] = total
        hold[i] = terms[pl.ds(pl.multiple_of(c * H, H), H), :]
        tu[pl.ds(pl.multiple_of(i * R, R), H), :] = terms[pl.ds(pl.multiple_of((1 - c) * H, H), H), :].astype(bf16)
        hop_core(i).start()

    def piece(k, base):
        return pl.ds(pl.multiple_of(base + k * PA, PA), PA)

    def stage1(zz):
        for xx in range(2):
            i = zz * 2 + xx
            hop_core(i).wait_recv()
            hold[i] = hold[i] + r_c[i].astype(f32)
        s_xa[zz] = hold[zz * 2 + 1 - x, 0:HA, :].astype(bf16)
        hop_xa(zz).start()
        for j in range(1, NY):
            y2, _ = to_y(j)
            for xx in range(2):
                s_yb[zz, j - 1, xx] = hold[zz * 2 + xx, piece(y2, HA), :].astype(bf16)
            hop_yb(zz, j).start()

    def stage2(zz):
        mine, other = zz * 2 + x, zz * 2 + 1 - x
        hop_xa(zz).wait_recv()
        hold[mine, 0:HA, :] = hold[mine, 0:HA, :] + r_xa[zz].astype(f32)
        for j in range(1, NY):
            y2, _ = to_y(j)
            s_ya[zz, j - 1] = hold[mine, piece(y2, 0), :].astype(bf16)
            hop_ya(zz, j).start()
        for j in range(1, NY):
            hop_yb(zz, j).wait_recv()
            for xx in range(2):
                at = piece(y, HA)
                hold[zz * 2 + xx, at, :] = hold[zz * 2 + xx, at, :] + r_yb[zz, j - 1, xx].astype(f32)
        s_xb[zz] = hold[other, piece(y, HA), :].astype(bf16)
        hop_xb(zz).start()

    def stage3(zz):
        mine = zz * 2 + x
        first, second = hold[mine, piece(y, 0), :], hold[mine, piece(y, HA), :]
        for j in range(1, NY):
            hop_ya(zz, j).wait_recv()
            first = first + r_ya[zz, j - 1].astype(f32)
        hop_xb(zz).wait_recv()
        second = second + r_xb[zz].astype(f32)

        @pl.when(zz == z)
        def _():
            own_z[0:PA, :] = first
            own_z[PA:2 * PA, :] = second

        for j in range(1, NZ):
            @pl.when(lax.rem(z + j, NZ) == zz)
            def _():
                s_z[j - 1, 0:PA, :] = first.astype(bf16)
                s_z[j - 1, PA:2 * PA, :] = second.astype(bf16)
                hop_z(j).start()

    def grad_step(t, _):
        grads(2 * t)
        grads(2 * t + 1)
        pl.when(t >= 1)(lambda: stage1(t - 1))
        pl.when(t >= 2)(lambda: stage2(t - 2))
        pl.when(t >= 3)(lambda: stage3(t - 3))
        return 0

    lax.fori_loop(0, NZ, grad_step, 0)

    def protos_of(k):
        def body(i, _):
            s = su[rows(i), :].astype(f32).T.astype(bf16)
            for n in range(0, M, NC):
                acc[:, n:n + NC] += jnp.dot(s, expl[rows(i), n:n + NC], preferred_element_type=f32)
            return 0

        lax.fori_loop(k * D // 4, (k + 1) * D // 4, body, 0)

    stage1(NZ - 1)
    stage2(NZ - 2)
    stage3(NZ - 3)
    protos_of(0)
    stage2(NZ - 1)
    stage3(NZ - 2)
    protos_of(1)
    stage3(NZ - 1)
    protos_of(2)
    total = own_z[...]
    for j in range(1, NZ):
        hop_z(j).wait_recv()
        total = total + r_z[j - 1].astype(f32)
    r_g[q] = total.astype(bf16)
    for j in range(1, Q):
        hop_g(j, q).start()
    protos_of(3)
    chunk = min(M, 256)
    for n in range(0, M, chunk):
        pg[n:n + chunk, :] = acc[:, n:n + chunk].T.astype(bf16)
    for j in range(1, Q):
        hop_g(j, q).wait_send()
        hop_g(j, lax.rem(q + Q - j, Q)).wait_recv()
    for k in range(Q):
        base = (k % 2) * H + (k // 2) * PA
        fg[base:base + PA, :] = r_g[k, 0:PA, :]
        fg[base + HA:base + HA + PA, :] = r_g[k, PA:2 * PA, :]

    w = su[rows(dp), :].astype(f32) * fg[...].astype(f32)
    sum_a[...] = w[:, 0:128]
    for k in range(128, K, 128):
        sum_a[...] += w[:, k:k + 128]
    own, off = place(dp)
    tot = fin[2, own, :, pl.ds(off + C, R)]
    mean = fin[2, own, :, pl.ds(off + 2 * C, R)] / tot
    loss[...] = jnp.log(tot) - (mean - lanes_to_row(sum_a) * (1.0 / (student_temp * factor)))

    def flushed(zz, _):
        hop_core(zz * 2).wait_send()
        hop_core(zz * 2 + 1).wait_send()
        hop_xa(zz).wait_send()
        hop_xb(zz).wait_send()
        for j in range(1, NY):
            hop_yb(zz, j).wait_send()
            hop_ya(zz, j).wait_send()
        return 0

    lax.fori_loop(0, NZ, flushed, 0)
    for j in range(1, NZ):
        hop_z(j).wait_send()
    sent(1)


def local(teacher_feat, student_feat, teacher_protos, student_protos):
    D, Q = lax.axis_size("dp"), lax.axis_size("proto")
    R, K = teacher_feat.shape
    M = teacher_protos.shape[0] // D
    B = D * R
    NZ, PS = D // 2, 2 * Q
    C = B // PS
    V = 3 * C
    hops = PS - 1 + NZ - 1 + PS - 1
    vmem = pl.BlockSpec(memory_space=pltpu.VMEM)
    hbm = pl.BlockSpec(memory_space=pl.ANY)
    NY = Q // 2
    H = R // 2
    HA = H // 2
    PA = HA // NY
    waits = D + NZ * (2 * NY + 1) + Q - 1
    loss, grad, proto_grad = pl.pallas_call(
        functools.partial(kernel, D, Q),
        out_shape=(
            jax.ShapeDtypeStruct((1, R), f32),
            jax.ShapeDtypeStruct((R, K), bf16),
            jax.ShapeDtypeStruct((M, K), bf16),
        ),
        in_specs=[vmem, vmem, hbm, hbm],
        out_specs=(vmem, vmem, vmem),
        scratch_shapes=[
            pltpu.VMEM((M, K), bf16),
            pltpu.VMEM((M, K), bf16),
            pltpu.VMEM((K, M), bf16),
            pltpu.VMEM((K, M), bf16),
            pltpu.VMEM((R, 128), f32),
            pltpu.VMEM((R, 128), f32),
            pltpu.VMEM((B, K), bf16),
            pltpu.VMEM((B, K), bf16),
            pltpu.VMEM((B, M), bf16),
            pltpu.VMEM((B, M), bf16),
            pltpu.VMEM((K, M), f32),
            pltpu.VMEM((1, M), f32),
            pltpu.VMEM((ITERS, PS, 1, V), f32),
            pltpu.VMEM((ITERS, 1, V), f32),
            pltpu.VMEM((ITERS, PS - 1, 1, V), f32),
            pltpu.VMEM((ITERS, NZ - 1, 1, V), f32),
            pltpu.VMEM((ITERS, PS, 1, V), f32),
            pltpu.VMEM((R, K), f32),
            pltpu.VMEM((D, H, K), f32),
            pltpu.VMEM((D, H, K), bf16),
            pltpu.VMEM((NZ, HA, K), bf16),
            pltpu.VMEM((NZ, HA, K), bf16),
            pltpu.VMEM((NZ, NY - 1, 2, PA, K), bf16),
            pltpu.VMEM((NZ, NY - 1, 2, PA, K), bf16),
            pltpu.VMEM((NZ, NY - 1, PA, K), bf16),
            pltpu.VMEM((NZ, NY - 1, PA, K), bf16),
            pltpu.VMEM((NZ, PA, K), bf16),
            pltpu.VMEM((NZ, PA, K), bf16),
            pltpu.VMEM((NZ - 1, 2 * PA, K), bf16),
            pltpu.VMEM((NZ - 1, 2 * PA, K), bf16),
            pltpu.VMEM((2 * PA, K), f32),
            pltpu.VMEM((Q, 2 * PA, K), bf16),
            pltpu.SemaphoreType.DMA((2,)),
            pltpu.SemaphoreType.DMA((2, 4, D)),
            pltpu.SemaphoreType.DMA((2, D, 2)),
            pltpu.SemaphoreType.DMA((ITERS, hops)),
            pltpu.SemaphoreType.DMA((ITERS, hops)),
            pltpu.SemaphoreType.DMA((waits,)),
            pltpu.SemaphoreType.DMA((waits,)),
        ],
        compiler_params=pltpu.CompilerParams(
            collective_id=0, has_side_effects=True, vmem_limit_bytes=62 * 2**20
        ),
    )(teacher_feat, student_feat, teacher_protos, student_protos)
    return loss.reshape(R), grad, proto_grad


def solution(mesh):
    placed = (P("dp", None), P("dp", None), P("proto", None), P("proto", None))
    return jax.shard_map(
        local,
        mesh=mesh,
        in_specs=placed,
        out_specs=(P("dp"), P("dp", None), P(("proto", "dp"), None)),
        check_vma=False,
    )
```
